256 devices in a mesh: section: 16 (over z_lo, y, core), peer: 16 (over z_hi, x).
Axes of the slice: x: 4, y: 4, z: 8 (z_hi: 4, z_lo: 2; z = z_hi * 2 + z_lo), core: 2. Of those that a mesh axis runs over, the one named last changes fastest.
Arguments:
- forward_inputs: bfloat16 [16, 16, 8, 16, 5120], P('section', 'peer'), may hold values from -6 to 6
- saved_inputs: bfloat16 [16, 16, 8, 16, 5120], P('section', 'peer'), may hold values from -6 to 6
- cotangents: bfloat16 [16, 16, 8, 16, 5120], P('section', 'peer'), may hold values from -6 to 6
- lengths: int32 [16, 16, 8], P('section', 'peer'), may hold values from 1 to 16, 80 in all within a row
- peer_counts: int32 [16], replicated, may hold values from 8 to 16, as said below
- wiring: int32 [16, 16, 8], P('section', 'peer'), may hold values from 0 to 15, as said below
- back_wiring: int32 [16, 16, 8], P('section', 'peer'), may hold values from 0 to 15, as said below
- norm_gains: float32 [16, 2, 5120], P('section'), may hold values from 0.5 to 2
- in_weights: bfloat16 [16, 2, 5120, 256], P('section', None, 'peer'), may hold values from -0.078125 to 0.078125
- down_weights: bfloat16 [16, 2, 128, 5120], P('section', None, None, 'peer'), may hold values from -0.5 to 0.5
Outputs:
- forward_arrivals: bfloat16 [16, 16, 16, 16, 5120], P('section', 'peer')
- backward_arrivals: bfloat16 [16, 16, 16, 16, 5120], P('section', 'peer')
- grad_in: float32 [16, 2, 5120, 256], P('section', None, 'peer')
- grad_down: float32 [16, 2, 128, 5120], P('section', None, None, 'peer')
The draws below stay inside these ranges and needn't reach their ends.
Inputs may be any that keep to these rules, and one draw needn't show every extreme that they name: `peer_counts`: each section has its active peers first along peer; some section has 16 and some has 8. `wiring`: the 8 entries of one device are distinct active peers of the next section (of section 0 after the last section). `back_wiring`: the 8 entries of one device are distinct active peers of the previous section (of the last section before section 0).
All inputs are finite; a program needn't handle non-finite values.
Results may differ from the reference program's by a relative error of at most 0.02.
Values may be sent and summed in bfloat16 or wider, within the bound.
No kernel may reach another device: no remote copies, remote signals or barrier semaphores. Data moves between devices by JAX's collectives and lax.ppermute only.
A program may use at most 128 MiB of HBM per device.

```python
import math
import jax
import jax.numpy as jnp
import numpy as np
from jax import lax

D = 5120
RANK = 128
MBTOK = 16
MICRO = 8
N_SECTION = 16
N_PEER = 16


def peer_list(key):
    first, second = jax.random.split(key)
    counts = jax.random.randint(first, (N_SECTION,), MICRO, N_PEER + 1)
    order = jax.random.permutation(second, N_SECTION)
    counts = counts.at[order[0]].set(N_PEER)
    counts = counts.at[order[1]].set(MICRO)
    return counts.astype(jnp.int32)


def choose_peers(key, counts):
    scores = jax.random.randint(key, (N_SECTION, N_PEER, N_PEER), 0, 1 << 20)
    column = jnp.arange(N_PEER, dtype=jnp.int32)
    scores = scores * N_PEER + column[None, None, :]
    scores = jnp.where(column[None, None, :] < counts[:, None, None], scores, (1 << 28) + column[None, None, :])
    order = jnp.argsort(scores, axis=-1, stable=True)
    return order[:, :, :MICRO].astype(jnp.int32)


def draw_peer_counts(key, part):
    return peer_list(key)


def draw_wiring(key, part):
    counts = peer_list(key)
    key = jax.random.fold_in(key, 7)
    return choose_peers(key, jnp.roll(counts, -1))


def draw_back_wiring(key, part):
    counts = peer_list(key)
    key = jax.random.fold_in(key, 9)
    return choose_peers(key, jnp.roll(counts, 1))


def block_scale(key, extent, cuts, smallest, top_value):
    factor_of, own = 1.0, jax.random.fold_in(key, 6)
    for position, parts in cuts:
        draws = jnp.exp(jax.random.uniform(jax.random.fold_in(own, position), (parts,), jnp.float32, smallest / len(cuts), top_value / len(cuts)))
        factor_of = factor_of * jnp.repeat(draws, extent[position] // parts).reshape([-1 if axis == position else 1 for axis in range(len(extent))])
    return factor_of


def split_up(amount, total, limit, slope):
    portions = [(1 << 20) // math.isqrt(rank ** slope) + 1 for rank in range(2, amount + 1)]
    surplus, given = total - limit - (amount - 1), [1] * (amount - 1)
    while surplus > 0:
        movable = [i for i in range(amount - 1) if given[i] < limit]
        whole, remaining = sum([portions[i] for i in movable]), surplus
        for i in movable:
            extra = min(limit - given[i], max(1, remaining * portions[i] // whole), surplus)
            given[i] = given[i] + extra
            surplus = surplus - extra
    return np.array([limit] + given)


def ragged_sizes(rng, amount, total, reach, slope):
    if amount == 2:
        one = jax.random.randint(rng, (), max(1, total - reach), min(reach, total - 1) + 1)
        return jnp.stack([one, total - one])
    sizes = jnp.asarray(split_up(amount, total, reach, slope), jnp.int32)
    pairs = (amount - 1) // 2
    giver, sink = sizes[1:1 + 2 * pairs:2], sizes[2:2 + 2 * pairs:2]
    slack = jnp.minimum(giver - 1, reach - sink)
    moved = jax.random.randint(jax.random.fold_in(rng, 1), (pairs,), 0, 1 << 20) % (slack + 1)
    sizes = sizes.at[1:1 + 2 * pairs:2].set(giver - moved).at[2:2 + 2 * pairs:2].set(sink + moved)
    return sizes[jax.random.permutation(jax.random.fold_in(rng, 2), amount)]


def normal_values(stream_key, dims, scale, reach, pieces=(), held_as=jnp.bfloat16):
    drawn = scale * jax.random.normal(stream_key, dims, jnp.float32)
    if pieces:
        drawn = drawn * block_scale(stream_key, dims, pieces, -0.22, 0.18)
    return jnp.clip(drawn, -reach, reach).astype(held_as)


def setup_inputs(seed: int = 0) -> dict:
    splits = jax.random.split(jax.random.key(seed), 11)
    return {
        "forward_inputs": normal_values(splits[0], (N_SECTION, N_PEER, MICRO, MBTOK, D), 1.0, 6.0, ((0, 16), (1, 16))),
        "saved_inputs": normal_values(splits[1], (N_SECTION, N_PEER, MICRO, MBTOK, D), 1.0, 6.0, ((0, 16), (1, 16))),
        "cotangents": normal_values(splits[2], (N_SECTION, N_PEER, MICRO, MBTOK, D), 1.0, 6.0, ((0, 16), (1, 16))),
        "lengths": jax.vmap(lambda own: ragged_sizes(own, MICRO, (5 * MICRO * MBTOK) // 8, MBTOK, 2))(jax.random.split(splits[3], N_SECTION * N_PEER)).reshape((N_SECTION, N_PEER, MICRO)).astype(jnp.int32),
        "peer_counts": draw_peer_counts(jax.random.fold_in(splits[10], 71), 0),
        "wiring": draw_wiring(jax.random.fold_in(splits[10], 71), 0),
        "back_wiring": draw_back_wiring(jax.random.fold_in(splits[10], 71), 0),
        "norm_gains": jnp.clip(jnp.exp(math.log(2.0) - 1.3862944 * jax.random.uniform(splits[7], (N_SECTION, 2, D), jnp.float32) ** block_scale(splits[7], (N_SECTION, 2, D), ((0, 16),), -0.2, 0.2)), 0.5, 2.0),
        "in_weights": normal_values(splits[8], (N_SECTION, 2, D, 2 * RANK), D ** -0.5, 0.078125, ((0, 16), (2, 16))),
        "down_weights": normal_values(splits[9], (N_SECTION, 2, RANK, D), RANK ** -0.5, 0.5, ((0, 16), (3, 16))),
    }


EPS = 1e-05

def contract_rows(left, right):
    return lax.dot_general(left, right, (((0,), (0,)), ((), ())), preferred_element_type=jnp.float32)

def contract_cols(left, right):
    return lax.dot_general(left, right, (((1,), (1,)), ((), ())), preferred_element_type=jnp.float32)

def layer_forward(stream, gain, weight_in, weight_down):
    inverse = lax.rsqrt(lax.optimization_barrier(jnp.mean(stream * stream, axis=-1, keepdims=True)) + EPS)
    normed = stream * inverse
    scaled = (normed * gain).astype(jnp.bfloat16)
    projected = jnp.dot(scaled, weight_in, preferred_element_type=jnp.float32)
    width = weight_down.shape[0]
    upward = projected[:, :width]
    gating = projected[:, width:]
    hidden = (jax.nn.silu(gating) * upward).astype(jnp.bfloat16)
    stream_next = stream + jnp.dot(hidden, weight_down, preferred_element_type=jnp.float32)
    return (stream_next, (inverse, normed, scaled, upward, gating, hidden))

def layer_backward(cotangent, gain, weight_in, weight_down, saved):
    inverse, normed, scaled, upward, gating, hidden = saved
    cot_low = cotangent.astype(jnp.bfloat16)
    d_hidden = contract_cols(cot_low, weight_down)
    sigmoid = jax.nn.sigmoid(gating)
    d_upward = d_hidden * (gating * sigmoid)
    d_gating = d_hidden * upward * sigmoid * (1.0 + gating * (1.0 - sigmoid))
    d_projected = jnp.concatenate([d_upward, d_gating], axis=-1).astype(jnp.bfloat16)
    d_normed = contract_cols(d_projected, weight_in) * gain
    inner = lax.optimization_barrier(jnp.mean(d_normed * normed, axis=-1, keepdims=True))
    d_stream = cotangent + inverse * (d_normed - normed * inner)
    return (d_stream, cot_low, d_projected)

def section_forward(rows, gains, weights_in, weights_down):
    stream = rows.astype(jnp.float32)
    for depth in range(2):
        stream, unused = layer_forward(stream, gains[depth], weights_in[depth], weights_down[depth])
    return stream.astype(jnp.bfloat16)

def section_backward(rows, cotangent, gains, weights_in, weights_down):
    stream = rows.astype(jnp.float32)
    kept = []
    for depth in range(2):
        stream, saved = layer_forward(stream, gains[depth], weights_in[depth], weights_down[depth])
        kept.append(saved)
    scaled_list, cot_list, dproj_list, hidden_list = ([None, None], [None, None], [None, None], [None, None])
    for depth in (1, 0):
        cotangent, cot_low, d_projected = layer_backward(cotangent, gains[depth], weights_in[depth], weights_down[depth], kept[depth])
        scaled_list[depth] = kept[depth][2]
        hidden_list[depth] = kept[depth][5]
        cot_list[depth] = cot_low
        dproj_list[depth] = d_projected
    return (cotangent.astype(jnp.bfloat16), jnp.stack(scaled_list), jnp.stack(cot_list), jnp.stack(dproj_list), jnp.stack(hidden_list))

def reference(forward_inputs, saved_inputs, cotangents, lengths, peer_counts, wiring, back_wiring, norm_gains, in_weights, down_weights):
    positions = jnp.arange(MBTOK, dtype=jnp.int32)
    peer_ids = jnp.arange(N_PEER, dtype=jnp.int32)
    forward_list = []
    backward_list = []
    grad_in_list = []
    grad_down_list = []
    for section_id in range(N_SECTION):
        active = peer_ids < peer_counts[section_id]
        gains = norm_gains[section_id]
        weights_in = in_weights[section_id]
        weights_down = down_weights[section_id]
        outputs = section_forward(forward_inputs[section_id].reshape(N_PEER * MICRO * MBTOK, D), gains, weights_in, weights_down)
        outputs = outputs.reshape(N_PEER, MICRO, MBTOK, D)
        routing = ((wiring[section_id][:, :, None] == peer_ids[None, None, :]) & active[:, None, None]).astype(jnp.float32)
        sent = jnp.einsum('pmq,pmtd->qptd', routing, outputs.astype(jnp.float32)).astype(jnp.bfloat16)
        forward_list.append(sent)
        live = (positions[None, None, :] < lengths[section_id][:, :, None]) & active[:, None, None]
        cotangent = cotangents[section_id].astype(jnp.float32) * live[..., None].astype(jnp.float32)
        d_rows, scaled_all, cot_all, dproj_all, hidden_all = section_backward(saved_inputs[section_id].reshape(N_PEER * MICRO * MBTOK, D), cotangent.reshape(N_PEER * MICRO * MBTOK, D), gains, weights_in, weights_down)
        grad_in_list.append(jnp.stack([contract_rows(scaled_all[depth], dproj_all[depth]) for depth in range(2)]))
        grad_down_list.append(jnp.stack([contract_rows(hidden_all[depth], cot_all[depth]) for depth in range(2)]))
        d_rows = d_rows.reshape(N_PEER, MICRO, MBTOK, D)
        back_routing = ((back_wiring[section_id][:, :, None] == peer_ids[None, None, :]) & active[:, None, None]).astype(jnp.float32)
        back_sent = jnp.einsum('pmq,pmtd->qptd', back_routing, d_rows.astype(jnp.float32)).astype(jnp.bfloat16)
        backward_list.append(back_sent)
    empty = jnp.zeros((N_PEER, N_PEER, MBTOK, D), jnp.bfloat16)
    forward_arrivals = jnp.stack([empty] + forward_list[:-1])
    backward_arrivals = jnp.stack(backward_list[1:] + [empty])
    return (forward_arrivals, backward_arrivals, jnp.stack(grad_in_list), jnp.stack(grad_down_list))
```

```python
import functools

import jax
import jax.numpy as jnp
from jax import lax
from jax.experimental import pallas as pl
from jax.experimental.pallas import tpu as pltpu
from jax.sharding import PartitionSpec as P

EPS = 1e-05
ROW = 4


def move(array, dz, dx, ds=0):
    sections, peers = lax.axis_size("section"), lax.axis_size("peer")
    rows = peers // ROW
    pairs = []
    for s in range(sections):
        if not 0 <= s + ds < sections:
            continue
        for z in range(rows):
            for x in range(ROW):
                there = ((z + dz) % rows) * ROW + (x + dx) % ROW
                pairs.append((s * peers + z * ROW + x, (s + ds) * peers + there))
    return lax.ppermute(array, ("section", "peer"), pairs)


def along(axis, by):
    return (by, 0) if axis == "z" else (0, by)


def ring_gather(block, axis, dim):
    half = block.shape[dim] // 2
    low, high = slice(0, half), slice(half, None)
    ahead = move(block, *along(axis, 1))
    behind = move(block, *along(axis, -1))
    cut = lambda array, part: lax.slice_in_dim(array, part.start, part.stop, axis=dim)
    far_low = move(lax.slice_in_dim(ahead, 0, half, axis=dim), *along(axis, 1))
    far_high = move(lax.slice_in_dim(behind, half, 2 * half, axis=dim), *along(axis, -1))
    return [(0, 0, block), (-1, 0, ahead), (1, 0, behind), (2, 0, far_low), (2, half, far_high)]


def gather_piece(piece, pz, px, order):
    rows = piece.shape[0]
    first, second = order
    mine = {"z": pz, "x": px}
    lead = jnp.zeros((ROW,) + piece.shape, piece.dtype)
    for offset, row, block in ring_gather(piece, first, 0):
        lead = lax.dynamic_update_slice(lead, block[None], ((mine[first] + offset) % ROW, row, 0))
    updates = []
    for offset, row, block in ring_gather(lead, second, 1):
        where = (mine[second] + offset) % ROW
        if second == "x":
            updates.append((0, where, row, block[:, None]))
        else:
            updates.append((where, 0, row, block[None]))
    return updates


def gather_weights(both, pz, px):
    layers, rows, width = both.shape
    half = rows // 2
    full = [jnp.zeros((ROW, ROW, rows, width), both.dtype) for _ in range(layers)]
    plan = [(1, half, "xz"), (0, 0, "zx"), (0, half, "zx"), (1, 0, "zx")]
    for layer, start, order in plan:
        for z, x, row, block in gather_piece(both[layer, start : start + half], pz, px, order):
            full[layer] = lax.dynamic_update_slice(full[layer], block, (z, x, start + row, 0))
    return [array.reshape(ROW * ROW * rows, width) for array in full]


def ring_scatter(parts, axis, dim):
    far = parts(2)
    half = far.shape[dim] // 2
    first = lax.slice_in_dim(far, 0, half, axis=dim)
    last = lax.slice_in_dim(far, half, 2 * half, axis=dim)
    from_behind = move(first, *along(axis, 1))
    from_ahead = move(last, *along(axis, -1))
    ahead, behind = parts(1), parts(-1)
    f32 = jnp.float32
    low = lax.slice_in_dim(ahead, 0, half, axis=dim).astype(f32) + from_behind.astype(f32)
    high = lax.slice_in_dim(behind, half, 2 * half, axis=dim).astype(f32) + from_ahead.astype(f32)
    ahead = jnp.concatenate([low.astype(ahead.dtype), lax.slice_in_dim(ahead, half, 2 * half, axis=dim)], dim)
    behind = jnp.concatenate([lax.slice_in_dim(behind, 0, half, axis=dim), high.astype(behind.dtype)], dim)
    got_ahead = move(ahead, *along(axis, 1))
    got_behind = move(behind, *along(axis, -1))
    return parts(0).astype(f32) + got_ahead.astype(f32) + got_behind.astype(f32)


def reduce_scatter(partial, pz, px):
    rows = partial.shape[0] // (ROW * ROW)
    cube = partial.reshape(ROW, ROW, rows, partial.shape[1])

    def column(offset):
        return lax.dynamic_index_in_dim(cube, (px + offset) % ROW, 1, keepdims=False)

    summed = ring_scatter(column, "x", 1).astype(partial.dtype)

    def own(offset):
        return lax.dynamic_index_in_dim(summed, (pz + offset) % ROW, 0, keepdims=False)

    return ring_scatter(own, "z", 0)


def place_kernel(count, where_ref, *refs):
    step = pl.program_id(0)
    for i in range(count):

        @pl.when(step // ROW == i)
        def _(i=i):
            refs[count][...] = refs[i][...]


def place(blocks, where):
    count = len(blocks)
    unit = (1,) + blocks[0].shape[1:]

    def source(i):
        return lambda step, where_ref: (jnp.clip(step - i * ROW, 0, ROW - 1), 0, 0)

    return pl.pallas_call(
        functools.partial(place_kernel, count),
        out_shape=jax.ShapeDtypeStruct((count * ROW,) + unit[1:], blocks[0].dtype),
        grid_spec=pltpu.PrefetchScalarGridSpec(
            num_scalar_prefetch=1,
            grid=(count * ROW,),
            in_specs=[pl.BlockSpec(unit, source(i)) for i in range(count)],
            out_specs=pl.BlockSpec(unit, lambda step, where_ref: (where_ref[step], 0, 0)),
        ),
    )(where, *blocks)


def spread_kernel(index_ref, values_ref, *groups):
    for dz, group in enumerate(groups):
        for dx in range(ROW):
            index = index_ref[dz * ROW + dx]

            @pl.when(index >= 0)
            def _():
                group[dx] = values_ref[jnp.maximum(index, 0)]

            @pl.when(index < 0)
            def _():
                group[dx] = jnp.zeros(values_ref.shape[1:], values_ref.dtype)


def spread(values, targets, active, pz, px):
    column = jnp.arange(ROW, dtype=jnp.int32)
    names = ((pz + column[:, None]) % ROW) * ROW + (px + column[None, :]) % ROW
    table = (targets[:, None] == names.reshape(1, -1)) & active
    micro = jnp.arange(targets.shape[0], dtype=jnp.int32)
    index = jnp.max(jnp.where(table, micro[:, None], -1), axis=0)
    group = jax.ShapeDtypeStruct((ROW,) + values.shape[1:], values.dtype)
    return pl.pallas_call(
        spread_kernel,
        out_shape=[group] * ROW,
        in_specs=[pl.BlockSpec(memory_space=pltpu.SMEM), pl.BlockSpec(memory_space=pltpu.VMEM)],
        out_specs=[pl.BlockSpec(memory_space=pltpu.VMEM)] * ROW,
        compiler_params=pltpu.CompilerParams(vmem_limit_bytes=16 << 20),
    )(index, values)


def deliver(groups, pz, px, ds):
    held = [move(group, dz, 0, ds) for dz, group in enumerate(groups)]
    blocks = []
    for dx in range(ROW):
        block = jnp.stack([held[dz][dx] for dz in range(ROW)])
        blocks.append(block if dx == 0 else move(block, 0, dx))
    where = [
        ((pz - dz) % ROW) * ROW + (px - dx) % ROW for dx in range(ROW) for dz in range(ROW)
    ]
    return place(blocks, jnp.stack(where).astype(jnp.int32))


def contract_rows(left, right):
    return lax.dot_general(left, right, (((0,), (0,)), ((), ())), preferred_element_type=jnp.float32)


def contract_cols(left, right):
    return lax.dot_general(left, right, (((1,), (1,)), ((), ())), preferred_element_type=jnp.float32)


def layer_forward(stream, gain, weight):
    rank = weight.shape[1] // 3
    inverse = lax.rsqrt(jnp.mean(stream * stream, axis=-1, keepdims=True) + EPS)
    normed = stream * inverse
    scaled = (normed * gain).astype(jnp.bfloat16)
    projected = jnp.dot(scaled, weight, preferred_element_type=jnp.float32)
    upward = projected[:, :rank]
    gating = projected[:, rank : 2 * rank]
    hidden = (jax.nn.silu(gating) * upward).astype(jnp.bfloat16)
    padded = jnp.pad(hidden, ((0, 0), (2 * rank, 0)))
    stream_next = stream + contract_cols(padded, weight)
    return (stream_next, (inverse, normed, scaled, upward, gating, hidden))


def layer_backward(cotangent, gain, weight, saved):
    inverse, normed, scaled, upward, gating, hidden = saved
    rank = weight.shape[1] // 3
    cot_low = cotangent.astype(jnp.bfloat16)
    d_hidden = jnp.dot(cot_low, weight, preferred_element_type=jnp.float32)[:, 2 * rank :]
    sigmoid = jax.nn.sigmoid(gating)
    d_upward = d_hidden * (gating * sigmoid)
    d_gating = d_hidden * upward * sigmoid * (1.0 + gating * (1.0 - sigmoid))
    d_projected = jnp.concatenate([d_upward, d_gating], axis=-1).astype(jnp.bfloat16)
    padded = jnp.pad(d_projected, ((0, 0), (0, rank)))
    d_normed = contract_cols(padded, weight) * gain
    inner = jnp.mean(d_normed * normed, axis=-1, keepdims=True)
    d_stream = cotangent + inverse * (d_normed - normed * inner)
    grad = jnp.concatenate(
        [contract_rows(scaled, d_projected).astype(jnp.bfloat16), contract_rows(cot_low, hidden).astype(jnp.bfloat16)],
        axis=-1,
    )
    return (d_stream, grad)


def per_device(
    forward_inputs,
    saved_inputs,
    cotangents,
    lengths,
    peer_counts,
    wiring,
    back_wiring,
    norm_gains,
    in_weights,
    down_weights,
):
    section_id = lax.axis_index("section")
    peer_id = lax.axis_index("peer")
    pz, px = peer_id // ROW, peer_id % ROW
    active = peer_id < peer_counts[section_id]
    micro, slots, width = forward_inputs.shape[2:]
    depth = in_weights.shape[1]
    both = jnp.concatenate([in_weights[0], jnp.swapaxes(down_weights[0], 1, 2)], axis=-1)
    weights = gather_weights(both, pz, px)
    gains = norm_gains[0]

    stream = forward_inputs.reshape(micro * slots, width).astype(jnp.float32)
    for layer in range(depth):
        stream, _ = layer_forward(stream, gains[layer], weights[layer])
    outputs = stream.astype(jnp.bfloat16).reshape(micro, slots, width)
    groups = spread(outputs, wiring[0, 0], active, pz, px)
    groups, saved_inputs = lax.optimization_barrier((groups, saved_inputs))
    forward_arrived = deliver(groups, pz, px, 1)

    positions = jnp.arange(slots, dtype=jnp.int32)
    live = ((positions[None, :] < lengths[0, 0][:, None]) & active).astype(jnp.float32)
    cotangent = cotangents[0, 0].astype(jnp.float32) * live[:, :, None]
    cotangent = cotangent.reshape(micro * slots, width)
    stream = saved_inputs.reshape(micro * slots, width).astype(jnp.float32)
    kept = []
    for layer in range(depth):
        stream, saved = layer_forward(stream, gains[layer], weights[layer])
        kept.append(saved)
    grads = [None] * depth
    for layer in reversed(range(depth)):
        cotangent, partial = layer_backward(cotangent, gains[layer], weights[layer], kept[layer])
        grads[layer] = partial
    d_rows = cotangent.astype(jnp.bfloat16).reshape(micro, slots, width)
    backward_arrived = deliver(spread(d_rows, back_wiring[0, 0], active, pz, px), pz, px, -1)

    sums = [reduce_scatter(grads[layer], pz, px) for layer in range(depth)]
    rank = down_weights.shape[2]
    grad_in = jnp.stack([total[:, : 2 * rank] for total in sums])
    grad_down = jnp.stack([total[:, 2 * rank :].T for total in sums])
    peers = ROW * ROW
    return (
        forward_arrived.reshape(1, 1, peers, slots, width),
        backward_arrived.reshape(1, 1, peers, slots, width),
        grad_in[None],
        grad_down[None],
    )


def solution(mesh):
    return jax.shard_map(
        per_device,
        mesh=mesh,
        in_specs=(
            P("section", "peer", None, None, None),
            P("section", "peer", None, None, None),
            P("section", "peer", None, None, None),
            P("section", "peer", None),
            P(),
            P("section", "peer", None),
            P("section", "peer", None),
            P("section", None, None),
            P("section", None, "peer", None),
            P("section", None, None, "peer"),
        ),
        out_specs=(
            P("section", "peer", None, None, None),
            P("section", "peer", None, None, None),
            P("section", None, "peer", None),
            P("section", None, None, "peer"),
        ),
        check_vma=False,
    )
```

```python
import functools

import jax
import jax.numpy as jnp
from jax import lax
from jax.experimental import pallas as pl
from jax.experimental.pallas import tpu as pltpu
from jax.sharding import PartitionSpec as P

EPS = 1e-05
CHUNK = 640
ROW = 4


def move(array, dz, dx, ds=0):
    sections, peers = lax.axis_size("section"), lax.axis_size("peer")
    rows = peers // ROW
    pairs = []
    for s in range(sections):
        if not 0 <= s + ds < sections:
            continue
        for z in range(rows):
            for x in range(ROW):
                there = ((z + dz) % rows) * ROW + (x + dx) % ROW
                pairs.append((s * peers + z * ROW + x, (s + ds) * peers + there))
    return lax.ppermute(array, ("section", "peer"), pairs)


def along(axis, by):
    return (by, 0) if axis == "z" else (0, by)


def ring_gather(block, axis):
    half = block.shape[0] // 2
    ahead = move(block, *along(axis, 1))
    behind = move(block, *along(axis, -1))
    far_low = move(ahead[:half], *along(axis, 1))
    far_high = move(behind[half:], *along(axis, -1))
    return [(0, 0, block), (-1, 0, ahead), (1, 0, behind), (2, 0, far_low), (2, half, far_high)]


OFFSETS = (0, -1, 1, 2)


def near_gather(piece, axis):
    return jnp.concatenate([piece] + [move(piece, *along(axis, -offset)) for offset in OFFSETS[1:]], axis=0)


def far_gather(lead, axis, parts):
    rows = lead.shape[0] // ROW
    held = []
    for far, row, block in ring_gather(lead, axis):
        spans = []
        for i in range(block.shape[0] // rows):
            near = OFFSETS[row // rows + i]
            dz, dx = (near, far) if axis == "x" else (far, near)
            at = i * rows
            for layer, start, count in parts:
                spans.append((at, dz, dx, layer, start, count))
                at += count
        held.append((block, spans))
    return held


def put_together(full_refs, refs, spans, where_ref, share, sems):
    copies = [[] for _ in full_refs]
    count = 0
    for ref, held in zip(refs, spans, strict=True):
        for row, dz, dx, layer, start, rows in held:
            z = lax.rem(where_ref[0] + (dz + ROW), ROW)
            x = lax.rem(where_ref[1] + (dx + ROW), ROW)
            there = pl.multiple_of((z * ROW + x) * share + start, 16)
            copy = pltpu.make_async_copy(
                ref.at[pl.ds(row, rows), :], full_refs[layer].at[pl.ds(there, rows), :], sems.at[count]
            )
            copy.start()
            copies[layer].append(copy)
            count += 1
    return copies


def wait_all(copies):
    for copy in copies:
        copy.wait()


def loop(steps, body, carry):
    for step in range(steps):
        carry = body(step, carry)
    return carry


def columns(step):
    return slice(step * CHUNK, (step + 1) * CHUNK)


def dot(left, right):
    return jnp.dot(left, right, preferred_element_type=jnp.float32)


def dot_cols(left, right):
    return lax.dot_general(left, right, (((1,), (1,)), ((), ())), preferred_element_type=jnp.float32)


def dot_rows(left, right):
    return lax.dot_general(left, right, (((0,), (0,)), ((), ())), preferred_element_type=jnp.float32)


def inverse_norm(stream_ref):
    rows, width = stream_ref.shape

    def add(step, total):
        part = stream_ref[:, columns(step)].astype(jnp.float32)
        return total + jnp.sum(part * part, axis=-1, keepdims=True)

    total = loop(width // CHUNK, add, jnp.zeros((rows, 1), jnp.float32))
    return lax.rsqrt(total / width + EPS)


def project(stream_ref, inverse, gain_ref, layer, full_ref):
    rows, width = stream_ref.shape
    rank = full_ref.shape[1] // 3

    def add(step, total):
        cols = columns(step)
        normed = stream_ref[:, cols].astype(jnp.float32) * inverse
        scaled = (normed * gain_ref[layer : layer + 1, cols]).astype(jnp.bfloat16)
        return total + dot(scaled, full_ref[cols, : 2 * rank])

    return loop(width // CHUNK, add, jnp.zeros((rows, 2 * rank), jnp.float32))


def gate(projected):
    rank = projected.shape[1] // 2
    upward, gating = projected[:, :rank], projected[:, rank:]
    sigmoid = jax.nn.sigmoid(gating)
    hidden = (gating * sigmoid * upward).astype(jnp.bfloat16)
    return upward, gating, sigmoid, hidden


def step_back(d_hidden, projected):
    upward, gating, sigmoid, hidden = gate(projected)
    d_upward = d_hidden * (gating * sigmoid)
    d_gating = d_hidden * upward * sigmoid * (1.0 + gating * (1.0 - sigmoid))
    return jnp.concatenate([d_upward, d_gating], axis=-1).astype(jnp.bfloat16), hidden


def hand_out(index_ref, rows_ref, routed_ref, slots):
    for peer in range(routed_ref.shape[0]):
        index = index_ref[peer]

        @pl.when(index >= 0)
        def _(index=index, peer=peer):
            start = pl.multiple_of(jnp.maximum(index, 0) * slots, slots)
            routed_ref[peer] = rows_ref[pl.ds(start, slots), :]

        @pl.when(index < 0)
        def _(peer=peer):
            routed_ref[peer] = jnp.zeros((slots, rows_ref.shape[1]), rows_ref.dtype)


def forward_kernel(spans, share, slots, where_ref, index_ref, gain_ref, input_ref, *refs):
    blocks = refs[: len(spans)]
    routed_ref, low_full_ref, high_full_ref, stream_ref, rows_ref, sems = refs[len(spans) :]
    copies = put_together((low_full_ref, high_full_ref), blocks, spans, where_ref, share, sems)
    rank = low_full_ref.shape[1] // 3
    steps = input_ref.shape[1] // CHUNK
    inverse = inverse_norm(input_ref)
    wait_all(copies[0])
    hidden = gate(project(input_ref, inverse, gain_ref, 0, low_full_ref))[3]

    def lower(step, total):
        cols = columns(step)
        new = input_ref[:, cols].astype(jnp.float32) + dot_cols(hidden, low_full_ref[cols, 2 * rank :])
        stream_ref[:, cols] = new
        return total + jnp.sum(new * new, axis=-1, keepdims=True)

    total = loop(steps, lower, jnp.zeros((input_ref.shape[0], 1), jnp.float32))
    inverse = lax.rsqrt(total / input_ref.shape[1] + EPS)
    wait_all(copies[1])
    hidden_high = gate(project(stream_ref, inverse, gain_ref, 1, high_full_ref))[3]

    def upper(step, carry):
        cols = columns(step)
        new = stream_ref[:, cols] + dot_cols(hidden_high, high_full_ref[cols, 2 * rank :])
        rows_ref[:, cols] = new.astype(jnp.bfloat16)
        return carry

    loop(steps, upper, 0)
    hand_out(index_ref, rows_ref, routed_ref, slots)


def spread_kernel(slots, index_ref, rows_ref, routed_ref):
    hand_out(index_ref, rows_ref, routed_ref, slots)


def back_kernel(spans, share, where_ref, gain_ref, saved_ref, cot_ref, *refs):
    blocks, refs = refs[: len(spans)], refs[len(spans) :]
    rows_ref, own_ref, up_ref, down_ref, next_ref, last_ref = refs[:6]
    low_full_ref, high_full_ref, stream_ref, scaled_ref, cot_low_ref, cot_high_ref, grad_ref, sems = refs[6:]
    copies = put_together((low_full_ref, high_full_ref), blocks, spans, where_ref, share, sems)
    count, width = saved_ref.shape
    rank = low_full_ref.shape[1] // 3
    steps = width // CHUNK
    f32, bf16 = jnp.float32, jnp.bfloat16
    nothing = jnp.zeros((count, rank), f32)

    inverse_low = inverse_norm(saved_ref)
    wait_all(copies[0])
    projected_low = project(saved_ref, inverse_low, gain_ref, 0, low_full_ref)
    hidden_low = gate(projected_low)[3]

    def first(step, total):
        cols = columns(step)
        new = saved_ref[:, cols].astype(f32) + dot_cols(hidden_low, low_full_ref[cols, 2 * rank :])
        stream_ref[:, cols] = new
        return total + jnp.sum(new * new, axis=-1, keepdims=True)

    total = loop(steps, first, jnp.zeros((count, 1), f32))
    inverse = lax.rsqrt(total / width + EPS)
    wait_all(copies[1])

    def forward(step, carry):
        projected, d_hidden = carry
        cols = columns(step)
        scaled = (stream_ref[:, cols] * inverse * gain_ref[1:2, cols]).astype(bf16)
        scaled_ref[:, cols] = scaled
        projected = projected + dot(scaled, high_full_ref[cols, : 2 * rank])
        d_hidden = d_hidden + dot(cot_ref[:, cols], high_full_ref[cols, 2 * rank :])
        return projected, d_hidden

    projected, d_hidden = loop(
        steps, forward, (jnp.zeros((count, 2 * rank), f32), nothing)
    )
    d_projected, hidden = step_back(d_hidden, projected)
    inner = jnp.sum(d_projected.astype(f32) * projected, axis=-1, keepdims=True) / width

    def store_grad(layer, step, scaled, cot_low, d_projected, hidden):
        peer = step * (CHUNK // share)
        wide = dot_rows(scaled, d_projected).astype(bf16)
        down = dot_rows(cot_low, hidden).astype(bf16)
        for i in range(CHUNK // share):
            grad_ref[layer, peer + i, :, : 2 * rank] = wide[i * share : (i + 1) * share]
            grad_ref[layer, peer + i, :, 2 * rank :] = down[i * share : (i + 1) * share]

    def upper(step, d_hidden_low):
        cols = columns(step)
        d_normed = dot_cols(d_projected, high_full_ref[cols, : 2 * rank]) * gain_ref[1:2, cols]
        normed = stream_ref[:, cols] * inverse
        cot_low = cot_ref[:, cols]
        new = cot_low.astype(f32) + inverse * (d_normed - normed * inner)
        cot_high_ref[:, cols] = new
        low = new.astype(bf16)
        cot_low_ref[:, cols] = low
        store_grad(1, step, scaled_ref[:, cols], cot_low, d_projected, hidden)
        return d_hidden_low + dot(low, low_full_ref[cols, 2 * rank :])

    d_hidden_low = loop(steps, upper, nothing)
    d_projected_low, _ = step_back(d_hidden_low, projected_low)
    inner_low = jnp.sum(d_projected_low.astype(f32) * projected_low, axis=-1, keepdims=True) / width

    def lower(step, carry):
        cols = columns(step)
        gain = gain_ref[0:1, cols]
        d_normed = dot_cols(d_projected_low, low_full_ref[cols, : 2 * rank]) * gain
        normed = saved_ref[:, cols].astype(f32) * inverse_low
        new = cot_high_ref[:, cols] + inverse_low * (d_normed - normed * inner_low)
        rows_ref[:, cols] = new.astype(bf16)
        scaled = (normed * gain).astype(bf16)
        store_grad(0, step, scaled, cot_low_ref[:, cols], d_projected_low, hidden_low)
        return carry

    loop(steps, lower, 0)

    half = share // 2
    for layer in range(2):
        for dz in range(ROW):
            z = lax.rem(where_ref[0] + dz, ROW) * ROW
            own, ahead, far, behind = (z + lax.rem(where_ref[1] + dx, ROW) for dx in range(ROW))
            own_ref[layer, dz] = grad_ref[layer, own]
            up_ref[0, layer, dz] = grad_ref[layer, far, :half]
            up_ref[1, layer, dz] = grad_ref[layer, ahead, half:]
            down_ref[0, layer, dz] = grad_ref[layer, far, half:]
            down_ref[1, layer, dz] = grad_ref[layer, behind, :half]
            next_ref[layer, dz] = grad_ref[layer, ahead, :half]
            last_ref[layer, dz] = grad_ref[layer, behind, half:]


def vmem(count):
    return [pl.BlockSpec(memory_space=pltpu.VMEM)] * count


def smem(count):
    return [pl.BlockSpec(memory_space=pltpu.SMEM)] * count


def shaped(*shape, dtype=jnp.bfloat16):
    return jax.ShapeDtypeStruct(shape, dtype)


def exchange(routed):
    return lax.all_to_all(routed, "peer", split_axis=0, concat_axis=0, tiled=True)


def slots_of(targets, active):
    names = jnp.arange(lax.axis_size("peer"), dtype=jnp.int32)
    table = (targets[:, None] == names[None, :]) & active
    micro = jnp.arange(targets.shape[0], dtype=jnp.int32)
    return jnp.max(jnp.where(table, micro[:, None], -1), axis=0)


def add_up(*terms):
    total = terms[0].astype(jnp.float32)
    for term in terms[1:]:
        total = total + term.astype(jnp.float32)
    return total


def scatter_first(up, down, axis):
    return move(up, *along(axis, 1)), move(down, *along(axis, -1))


def scatter_rest(own, ahead, behind, got_up, got_down, axis):
    half = ahead.shape[-2]
    ahead = add_up(ahead, got_up[0]).astype(own.dtype)
    behind = add_up(behind, got_down[0]).astype(own.dtype)
    ahead, behind = lax.optimization_barrier((ahead, behind))
    got_ahead, got_behind = move(ahead, *along(axis, 1)), move(behind, *along(axis, -1))
    low = add_up(own[..., :half, :], got_ahead, got_down[1])
    high = add_up(own[..., half:, :], got_behind, got_up[1])
    return low, high


def reduce_scatter(own, ahead, behind, got_up, got_down, after):
    dtype = own.dtype
    low, high = scatter_rest(own, ahead, behind, got_up, got_down, "x")
    low, high = low.astype(dtype), high.astype(dtype)
    up, down = scatter_first(
        jnp.stack([low[:, 2], high[:, 1]]), jnp.stack([high[:, 2], low[:, 3]]), "z"
    )
    mine = jnp.concatenate([low[:, 0], high[:, 0]], axis=1)
    low, high = scatter_rest(mine, low[:, 1], high[:, 3], up, down, "z")
    low, high, after = lax.optimization_barrier((low, high, after))
    return jnp.concatenate([low, high], axis=1), after


def cost(micros):
    return pl.CostEstimate(flops=micros * 10**9, bytes_accessed=micros * 3 * 10**6, transcendentals=0)


def per_device(
    forward_inputs,
    saved_inputs,
    cotangents,
    lengths,
    peer_counts,
    wiring,
    back_wiring,
    norm_gains,
    in_weights,
    down_weights,
):
    section_id = lax.axis_index("section")
    peer_id = lax.axis_index("peer")
    where = jnp.stack([peer_id // ROW, peer_id % ROW]).astype(jnp.int32)
    active = peer_id < peer_counts[section_id]
    micro, slots, width = forward_inputs.shape[2:]
    count = micro * slots
    rank = down_weights.shape[2]
    share = in_weights.shape[2]
    gains = norm_gains[0]
    f32 = jnp.float32

    both = jnp.concatenate([in_weights[0], jnp.swapaxes(down_weights[0], 1, 2)], axis=-1)
    cut = share * 45 // 100 // 16 * 16
    by_z = near_gather(jnp.concatenate([both[0], both[1, :cut]], axis=0), "z")
    by_x = near_gather(both[1, cut:], "x")
    by_z, by_x = lax.optimization_barrier((by_z, by_x))
    blocks = far_gather(by_z, "x", [(0, 0, share), (1, 0, cut)])
    blocks += far_gather(by_x, "z", [(1, cut, share - cut)])

    forward_slots = slots_of(wiring[0, 0], active)
    back_slots = move(slots_of(back_wiring[0, 0], active), 0, 0, -1)
    positions = jnp.arange(slots, dtype=jnp.int32)
    live = (positions[None, :] < lengths[0, 0][:, None]) & active
    cot = jnp.where(live[:, :, None], cotangents[0, 0], jnp.zeros((), cotangents.dtype))
    cot = cot.reshape(count, width)
    saved = saved_inputs.reshape(count, width)

    peers = ROW * ROW
    routed = shaped(peers, slots, width)
    flat = shaped(count, width)
    bf16 = jnp.bfloat16

    spans = [held for _, held in blocks]
    arrays = [array for array, _ in blocks]
    anywhere = [pl.BlockSpec(memory_space=pl.ANY)] * len(spans)
    wide = [pltpu.VMEM((width, 3 * rank), bf16)] * 2
    sems = pltpu.SemaphoreType.DMA((sum(len(held) for held in spans),))
    outgoing = pl.pallas_call(
        functools.partial(forward_kernel, spans, share, slots),
        out_shape=routed,
        in_specs=smem(2) + vmem(2) + anywhere,
        out_specs=vmem(1)[0],
        scratch_shapes=wide + [pltpu.VMEM((count, width), f32), pltpu.VMEM((count, width), bf16), sems],
        compiler_params=pltpu.CompilerParams(vmem_limit_bytes=40 << 20),
        cost_estimate=cost(12),
    )(where, forward_slots, gains, forward_inputs.reshape(count, width), *arrays)

    outgoing, saved = lax.optimization_barrier((outgoing, saved))
    forward_arrived = move(exchange(outgoing), 0, 0, 1)

    part = shaped(2, ROW, share // 2, 3 * rank)
    pair = shaped(2, 2, ROW, share // 2, 3 * rank)
    d_rows, own, up, down, ahead, behind = pl.pallas_call(
        functools.partial(back_kernel, spans, share),
        out_shape=[flat, shaped(2, ROW, share, 3 * rank), pair, pair, part, part],
        in_specs=smem(1) + vmem(3) + anywhere,
        out_specs=vmem(6),
        scratch_shapes=wide
        + [
            pltpu.VMEM((count, width), f32),
            pltpu.VMEM((count, width), bf16),
            pltpu.VMEM((count, width), bf16),
            pltpu.VMEM((count, width), f32),
            pltpu.VMEM((2, peers, share, 3 * rank), bf16),
            sems,
        ],
        compiler_params=pltpu.CompilerParams(vmem_limit_bytes=52 << 20),
        cost_estimate=cost(25),
    )(where, gains, saved, cot, *arrays)
    returned = pl.pallas_call(
        functools.partial(spread_kernel, slots),
        out_shape=routed,
        in_specs=smem(1) + vmem(1),
        out_specs=vmem(1)[0],
        compiler_params=pltpu.CompilerParams(vmem_limit_bytes=16 << 20),
        cost_estimate=cost(2),
    )(back_slots, move(d_rows, 0, 0, -1))
    got_up, got_down = scatter_first(up, down, "x")
    returned, got_up, got_down = lax.optimization_barrier((returned, got_up, got_down))
    backward_arrived = exchange(returned)
    total, forward_arrived = reduce_scatter(own, ahead, behind, got_up, got_down, forward_arrived)

    grad_in = total[:, :, : 2 * rank]
    grad_down = jnp.swapaxes(total[:, :, 2 * rank :], 1, 2)
    return (
        forward_arrived.reshape(1, 1, peers, slots, width),
        backward_arrived.reshape(1, 1, peers, slots, width),
        grad_in[None],
        grad_down[None],
    )


def solution(mesh):
    return jax.shard_map(
        per_device,
        mesh=mesh,
        in_specs=(
            P("section", "peer", None, None, None),
            P("section", "peer", None, None, None),
            P("section", "peer", None, None, None),
            P("section", "peer", None),
            P(),
            P("section", "peer", None),
            P("section", "peer", None),
            P("section", None, None),
            P("section", None, "peer", None),
            P("section", None, None, "peer"),
        ),
        out_specs=(
            P("section", "peer", None, None, None),
            P("section", "peer", None, None, None),
            P("section", None, "peer", None),
            P("section", None, None, "peer"),
        ),
        check_vma=False,
    )
```

```python
import functools

import jax
import jax.numpy as jnp
from jax import lax
from jax.experimental import pallas as pl
from jax.experimental.pallas import tpu as pltpu
from jax.sharding import PartitionSpec as P

EPS = 1e-05
CHUNK = 640
ROW = 4


def move(array, dz, dx, ds=0):
    sections, peers = lax.axis_size("section"), lax.axis_size("peer")
    rows = peers // ROW
    pairs = []
    for s in range(sections):
        if not 0 <= s + ds < sections:
            continue
        for z in range(rows):
            for x in range(ROW):
                there = ((z + dz) % rows) * ROW + (x + dx) % ROW
                pairs.append((s * peers + z * ROW + x, (s + ds) * peers + there))
    return lax.ppermute(array, ("section", "peer"), pairs)


def along(axis, by):
    return (by, 0) if axis == "z" else (0, by)


def ring_gather(block, axis):
    half = block.shape[0] // 2
    ahead = move(block, *along(axis, 1))
    behind = move(block, *along(axis, -1))
    far_low = move(ahead[:half], *along(axis, 1))
    far_high = move(behind[half:], *along(axis, -1))
    return [(0, 0, block), (-1, 0, ahead), (1, 0, behind), (2, 0, far_low), (2, half, far_high)]


OFFSETS = (0, -1, 1, 2)


def near_gather(piece, axis):
    return jnp.concatenate([piece] + [move(piece, *along(axis, -offset)) for offset in OFFSETS[1:]], axis=0)


def far_gather(lead, axis, parts):
    rows = lead.shape[0] // ROW
    held = []
    for far, row, block in ring_gather(lead, axis):
        spans = []
        for i in range(block.shape[0] // rows):
            near = OFFSETS[row // rows + i]
            dz, dx = (near, far) if axis == "x" else (far, near)
            at = i * rows
            for layer, start, count in parts:
                spans.append((at, dz, dx, layer, start, count))
                at += count
        held.append((block, spans))
    return held


def put_together(full_refs, refs, spans, where_ref, share, sems):
    copies = [[] for _ in full_refs]
    count = 0
    for ref, held in zip(refs, spans, strict=True):
        for row, dz, dx, layer, start, rows in held:
            z = lax.rem(where_ref[0] + (dz + ROW), ROW)
            x = lax.rem(where_ref[1] + (dx + ROW), ROW)
            there = pl.multiple_of((z * ROW + x) * share + start, 16)
            copy = pltpu.make_async_copy(
                ref.at[pl.ds(row, rows), :], full_refs[layer].at[pl.ds(there, rows), :], sems.at[count]
            )
            copy.start()
            copies[layer].append(copy)
            count += 1
    return copies


def wait_all(copies):
    for copy in copies:
        copy.wait()


def loop(steps, body, carry):
    for step in range(steps):
        carry = body(step, carry)
    return carry


def columns(step):
    return slice(step * CHUNK, (step + 1) * CHUNK)


def dot(left, right):
    return jnp.dot(left, right, preferred_element_type=jnp.float32)


def dot_cols(left, right):
    return lax.dot_general(left, right, (((1,), (1,)), ((), ())), preferred_element_type=jnp.float32)


def dot_rows(left, right):
    return lax.dot_general(left, right, (((0,), (0,)), ((), ())), preferred_element_type=jnp.float32)


def inverse_norm(stream_ref):
    rows, width = stream_ref.shape

    def add(step, total):
        part = stream_ref[:, columns(step)].astype(jnp.float32)
        return total + jnp.sum(part * part, axis=-1, keepdims=True)

    total = loop(width // CHUNK, add, jnp.zeros((rows, 1), jnp.float32))
    return lax.rsqrt(total / width + EPS)


def project(stream_ref, inverse, gain_ref, layer, full_ref):
    rows, width = stream_ref.shape
    rank = full_ref.shape[1] // 3

    def add(step, total):
        cols = columns(step)
        normed = stream_ref[:, cols].astype(jnp.float32) * inverse
        scaled = (normed * gain_ref[layer : layer + 1, cols]).astype(jnp.bfloat16)
        return total + dot(scaled, full_ref[cols, : 2 * rank])

    return loop(width // CHUNK, add, jnp.zeros((rows, 2 * rank), jnp.float32))


def gate(projected):
    rank = projected.shape[1] // 2
    upward, gating = projected[:, :rank], projected[:, rank:]
    sigmoid = jax.nn.sigmoid(gating)
    hidden = (gating * sigmoid * upward).astype(jnp.bfloat16)
    return upward, gating, sigmoid, hidden


def step_back(d_hidden, projected):
    upward, gating, sigmoid, hidden = gate(projected)
    d_upward = d_hidden * (gating * sigmoid)
    d_gating = d_hidden * upward * sigmoid * (1.0 + gating * (1.0 - sigmoid))
    return jnp.concatenate([d_upward, d_gating], axis=-1).astype(jnp.bfloat16), hidden


def hand_out(index_ref, rows_ref, routed_ref, slots):
    for peer in range(routed_ref.shape[0]):
        index = index_ref[peer]

        @pl.when(index >= 0)
        def _(index=index, peer=peer):
            start = pl.multiple_of(jnp.maximum(index, 0) * slots, slots)
            routed_ref[peer] = rows_ref[pl.ds(start, slots), :]

        @pl.when(index < 0)
        def _(peer=peer):
            routed_ref[peer] = jnp.zeros((slots, rows_ref.shape[1]), rows_ref.dtype)


def forward_kernel(spans, share, where_ref, gain_ref, input_ref, *refs):
    blocks = refs[: len(spans)]
    rows_ref, low_full_ref, high_full_ref, stream_ref, sems = refs[len(spans) :]
    copies = put_together((low_full_ref, high_full_ref), blocks, spans, where_ref, share, sems)
    rank = low_full_ref.shape[1] // 3
    steps = input_ref.shape[1] // CHUNK
    inverse = inverse_norm(input_ref)
    wait_all(copies[0])
    hidden = gate(project(input_ref, inverse, gain_ref, 0, low_full_ref))[3]

    def lower(step, total):
        cols = columns(step)
        new = input_ref[:, cols].astype(jnp.float32) + dot_cols(hidden, low_full_ref[cols, 2 * rank :])
        stream_ref[:, cols] = new
        return total + jnp.sum(new * new, axis=-1, keepdims=True)

    total = loop(steps, lower, jnp.zeros((input_ref.shape[0], 1), jnp.float32))
    inverse = lax.rsqrt(total / input_ref.shape[1] + EPS)
    wait_all(copies[1])
    hidden_high = gate(project(stream_ref, inverse, gain_ref, 1, high_full_ref))[3]

    def upper(step, carry):
        cols = columns(step)
        new = stream_ref[:, cols] + dot_cols(hidden_high, high_full_ref[cols, 2 * rank :])
        rows_ref[:, cols] = new.astype(jnp.bfloat16)
        return carry

    loop(steps, upper, 0)


def spread_kernel(slots, index_ref, rows_ref, routed_ref):
    hand_out(index_ref, rows_ref, routed_ref, slots)


def back_kernel(spans, share, where_ref, gain_ref, saved_ref, cot_ref, *refs):
    blocks, refs = refs[: len(spans)], refs[len(spans) :]
    rows_ref, own_ref, up_ref, down_ref, next_ref, last_ref = refs[:6]
    low_full_ref, high_full_ref, stream_ref, scaled_ref, cot_low_ref, cot_high_ref, grad_ref, sems = refs[6:]
    copies = put_together((low_full_ref, high_full_ref), blocks, spans, where_ref, share, sems)
    count, width = saved_ref.shape
    rank = low_full_ref.shape[1] // 3
    steps = width // CHUNK
    f32, bf16 = jnp.float32, jnp.bfloat16
    nothing = jnp.zeros((count, rank), f32)

    inverse_low = inverse_norm(saved_ref)
    wait_all(copies[0])
    projected_low = project(saved_ref, inverse_low, gain_ref, 0, low_full_ref)
    hidden_low = gate(projected_low)[3]

    def first(step, total):
        cols = columns(step)
        new = saved_ref[:, cols].astype(f32) + dot_cols(hidden_low, low_full_ref[cols, 2 * rank :])
        stream_ref[:, cols] = new
        return total + jnp.sum(new * new, axis=-1, keepdims=True)

    total = loop(steps, first, jnp.zeros((count, 1), f32))
    inverse = lax.rsqrt(total / width + EPS)
    wait_all(copies[1])

    def forward(step, carry):
        projected, d_hidden = carry
        cols = columns(step)
        scaled = (stream_ref[:, cols] * inverse * gain_ref[1:2, cols]).astype(bf16)
        scaled_ref[:, cols] = scaled
        projected = projected + dot(scaled, high_full_ref[cols, : 2 * rank])
        d_hidden = d_hidden + dot(cot_ref[:, cols], high_full_ref[cols, 2 * rank :])
        return projected, d_hidden

    projected, d_hidden = loop(
        steps, forward, (jnp.zeros((count, 2 * rank), f32), nothing)
    )
    d_projected, hidden = step_back(d_hidden, projected)
    inner = jnp.sum(d_projected.astype(f32) * projected, axis=-1, keepdims=True) / width

    def store_grad(layer, step, scaled, cot_low, d_projected, hidden):
        peer = step * (CHUNK // share)
        wide = dot_rows(scaled, d_projected).astype(bf16)
        down = dot_rows(cot_low, hidden).astype(bf16)
        for i in range(CHUNK // share):
            grad_ref[layer, peer + i, :, : 2 * rank] = wide[i * share : (i + 1) * share]
            grad_ref[layer, peer + i, :, 2 * rank :] = down[i * share : (i + 1) * share]

    def upper(step, d_hidden_low):
        cols = columns(step)
        d_normed = dot_cols(d_projected, high_full_ref[cols, : 2 * rank]) * gain_ref[1:2, cols]
        normed = stream_ref[:, cols] * inverse
        cot_low = cot_ref[:, cols]
        new = cot_low.astype(f32) + inverse * (d_normed - normed * inner)
        cot_high_ref[:, cols] = new
        low = new.astype(bf16)
        cot_low_ref[:, cols] = low
        store_grad(1, step, scaled_ref[:, cols], cot_low, d_projected, hidden)
        return d_hidden_low + dot(low, low_full_ref[cols, 2 * rank :])

    d_hidden_low = loop(steps, upper, nothing)
    d_projected_low, _ = step_back(d_hidden_low, projected_low)
    inner_low = jnp.sum(d_projected_low.astype(f32) * projected_low, axis=-1, keepdims=True) / width

    def lower(step, carry):
        cols = columns(step)
        gain = gain_ref[0:1, cols]
        d_normed = dot_cols(d_projected_low, low_full_ref[cols, : 2 * rank]) * gain
        normed = saved_ref[:, cols].astype(f32) * inverse_low
        new = cot_high_ref[:, cols] + inverse_low * (d_normed - normed * inner_low)
        rows_ref[:, cols] = new.astype(bf16)
        scaled = (normed * gain).astype(bf16)
        store_grad(0, step, scaled, cot_low_ref[:, cols], d_projected_low, hidden_low)
        return carry

    loop(steps, lower, 0)

    half = share // 2
    for layer in range(2):
        for dz in range(ROW):
            z = lax.rem(where_ref[0] + dz, ROW) * ROW
            own, ahead, far, behind = (z + lax.rem(where_ref[1] + dx, ROW) for dx in range(ROW))
            own_ref[dz, layer] = grad_ref[layer, own]
            up_ref[0, dz, layer] = grad_ref[layer, far, :half]
            up_ref[1, dz, layer] = grad_ref[layer, ahead, half:]
            down_ref[0, dz, layer] = grad_ref[layer, far, half:]
            down_ref[1, dz, layer] = grad_ref[layer, behind, :half]
            next_ref[dz, layer] = grad_ref[layer, ahead, :half]
            last_ref[dz, layer] = grad_ref[layer, behind, half:]


def vmem(count):
    return [pl.BlockSpec(memory_space=pltpu.VMEM)] * count


def smem(count):
    return [pl.BlockSpec(memory_space=pltpu.SMEM)] * count


def shaped(*shape, dtype=jnp.bfloat16):
    return jax.ShapeDtypeStruct(shape, dtype)


def exchange(routed):
    return lax.all_to_all(routed, "peer", split_axis=0, concat_axis=0, tiled=True)


def settle_kernel(from_ref, to_ref):
    to_ref[...] = from_ref[...]


def settle(array):
    step = pl.BlockSpec((2,) + array.shape[1:], lambda i: (i, 0, 0))
    return pl.pallas_call(
        settle_kernel,
        out_shape=jax.ShapeDtypeStruct(array.shape, array.dtype),
        grid=(array.shape[0] // 2,),
        in_specs=[step],
        out_specs=step,
        cost_estimate=cost(3),
    )(array)


def slots_of(targets, active):
    names = jnp.arange(lax.axis_size("peer"), dtype=jnp.int32)
    table = (targets[:, None] == names[None, :]) & active
    micro = jnp.arange(targets.shape[0], dtype=jnp.int32)
    return jnp.max(jnp.where(table, micro[:, None], -1), axis=0)


def add_up(*terms):
    total = terms[0].astype(jnp.float32)
    for term in terms[1:]:
        total = total + term.astype(jnp.float32)
    return total


def scatter_first(up, down, axis):
    return move(up, *along(axis, 1)), move(down, *along(axis, -1))


def scatter_rest(own, ahead, behind, got_up, got_down, axis):
    half = ahead.shape[-2]
    ahead = add_up(ahead, got_up[0]).astype(own.dtype)
    behind = add_up(behind, got_down[0]).astype(own.dtype)
    ahead, behind = lax.optimization_barrier((ahead, behind))
    got_ahead, got_behind = move(ahead, *along(axis, 1)), move(behind, *along(axis, -1))
    low = add_up(own[..., :half, :], got_ahead, got_down[1])
    high = add_up(own[..., half:, :], got_behind, got_up[1])
    return low, high


def reduce_scatter(own, ahead, behind, got_up, got_down, after):
    dtype = own.dtype
    low, high = scatter_rest(own, ahead, behind, got_up, got_down, "x")
    low, high = low.astype(dtype), high.astype(dtype)
    up, down = scatter_first(jnp.stack([low[2], high[1]]), jnp.stack([high[2], low[3]]), "z")
    up, down, after = lax.optimization_barrier((up, down, after))
    mine = jnp.concatenate([low[0], high[0]], axis=1)
    return jnp.concatenate(scatter_rest(mine, low[1], high[3], up, down, "z"), axis=1), after


def cost(micros):
    return pl.CostEstimate(flops=micros * 10**9, bytes_accessed=micros * 3 * 10**6, transcendentals=0)


def per_device(
    forward_inputs,
    saved_inputs,
    cotangents,
    lengths,
    peer_counts,
    wiring,
    back_wiring,
    norm_gains,
    in_weights,
    down_weights,
):
    section_id = lax.axis_index("section")
    peer_id = lax.axis_index("peer")
    where = jnp.stack([peer_id // ROW, peer_id % ROW]).astype(jnp.int32)
    active = peer_id < peer_counts[section_id]
    micro, slots, width = forward_inputs.shape[2:]
    count = micro * slots
    rank = down_weights.shape[2]
    share = in_weights.shape[2]
    gains = norm_gains[0]
    f32 = jnp.float32

    both = jnp.concatenate([in_weights[0], jnp.swapaxes(down_weights[0], 1, 2)], axis=-1)
    cut = share * 45 // 100 // 16 * 16
    by_z = near_gather(jnp.concatenate([both[0], both[1, :cut]], axis=0), "z")
    by_x = near_gather(both[1, cut:], "x")
    forward_slots = move(slots_of(wiring[0, 0], active), 0, 0, 1)
    back_slots = move(slots_of(back_wiring[0, 0], active), 0, 0, -1)
    by_z, by_x, forward_slots, back_slots = lax.optimization_barrier((by_z, by_x, forward_slots, back_slots))
    blocks = far_gather(by_z, "x", [(0, 0, share), (1, 0, cut)])
    blocks += far_gather(by_x, "z", [(1, cut, share - cut)])

    positions = jnp.arange(slots, dtype=jnp.int32)
    live = (positions[None, :] < lengths[0, 0][:, None]) & active
    cot = jnp.where(live[:, :, None], cotangents[0, 0], jnp.zeros((), cotangents.dtype))
    cot = cot.reshape(count, width)
    saved = saved_inputs.reshape(count, width)

    peers = ROW * ROW
    routed = shaped(peers, slots, width)
    flat = shaped(count, width)
    bf16 = jnp.bfloat16

    spans = [held for _, held in blocks]
    arrays = [array for array, _ in blocks]
    anywhere = [pl.BlockSpec(memory_space=pl.ANY)] * len(spans)
    wide = [pltpu.VMEM((width, 3 * rank), bf16)] * 2
    sems = pltpu.SemaphoreType.DMA((sum(len(held) for held in spans),))
    def spread(index, rows):
        return pl.pallas_call(
            functools.partial(spread_kernel, slots),
            out_shape=routed,
            in_specs=smem(1) + vmem(1),
            out_specs=vmem(1)[0],
            compiler_params=pltpu.CompilerParams(vmem_limit_bytes=16 << 20),
            cost_estimate=cost(2),
        )(index, rows)

    part = shaped(ROW, 2, share // 2, 3 * rank)
    pair = shaped(2, ROW, 2, share // 2, 3 * rank)
    d_rows, own, up, down, ahead, behind = pl.pallas_call(
        functools.partial(back_kernel, spans, share),
        out_shape=[flat, shaped(ROW, 2, share, 3 * rank), pair, pair, part, part],
        in_specs=smem(1) + vmem(3) + anywhere,
        out_specs=vmem(6),
        scratch_shapes=wide
        + [
            pltpu.VMEM((count, width), f32),
            pltpu.VMEM((count, width), bf16),
            pltpu.VMEM((count, width), bf16),
            pltpu.VMEM((count, width), f32),
            pltpu.VMEM((2, peers, share, 3 * rank), bf16),
            sems,
        ],
        compiler_params=pltpu.CompilerParams(vmem_limit_bytes=52 << 20),
        cost_estimate=cost(25),
    )(where, gains, saved, cot, *arrays)
    d_rows, up, down, inputs = lax.optimization_barrier(
        (d_rows, up, down, forward_inputs.reshape(count, width))
    )
    got_up, got_down = scatter_first(up, down, "x")
    shifted = move(d_rows, 0, 0, -1)
    rows = pl.pallas_call(
        functools.partial(forward_kernel, spans, share),
        out_shape=flat,
        in_specs=smem(1) + vmem(2) + anywhere,
        out_specs=vmem(1)[0],
        scratch_shapes=wide + [pltpu.VMEM((count, width), f32), sems],
        compiler_params=pltpu.CompilerParams(vmem_limit_bytes=40 << 20),
        cost_estimate=cost(12),
    )(where, gains, inputs, *arrays)

    shifted, rows = lax.optimization_barrier((shifted, rows))
    backward_arrived = settle(exchange(spread(back_slots, shifted)))
    outgoing = spread(forward_slots, move(rows, 0, 0, 1))
    outgoing, got_up, got_down = lax.optimization_barrier((outgoing, got_up, got_down))
    forward_arrived = exchange(outgoing)
    total, backward_arrived = reduce_scatter(own, ahead, behind, got_up, got_down, backward_arrived)

    grad_in = total[:, :, : 2 * rank]
    grad_down = jnp.swapaxes(total[:, :, 2 * rank :], 1, 2)
    return (
        forward_arrived.reshape(1, 1, peers, slots, width),
        backward_arrived.reshape(1, 1, peers, slots, width),
        grad_in[None],
        grad_down[None],
    )


def solution(mesh):
    return jax.shard_map(
        per_device,
        mesh=mesh,
        in_specs=(
            P("section", "peer", None, None, None),
            P("section", "peer", None, None, None),
            P("section", "peer", None, None, None),
            P("section", "peer", None),
            P(),
            P("section", "peer", None),
            P("section", "peer", None),
            P("section", None, None),
            P("section", None, "peer", None),
            P("section", None, None, "peer"),
        ),
        out_specs=(
            P("section", "peer", None, None, None),
            P("section", "peer", None, None, None),
            P("section", None, "peer", None),
            P("section", None, None, "peer"),
        ),
        check_vma=False,
    )
```

```python
import functools

import jax
import jax.numpy as jnp
from jax import lax
from jax.experimental import pallas as pl
from jax.experimental.pallas import tpu as pltpu
from jax.sharding import PartitionSpec as P

EPS = 1e-05
CHUNK = 640
ROW = 4


def move(array, dz, dx, ds=0):
    sections, peers = lax.axis_size("section"), lax.axis_size("peer")
    rows = peers // ROW
    pairs = []
    for s in range(sections):
        if not 0 <= s + ds < sections:
            continue
        for z in range(rows):
            for x in range(ROW):
                there = ((z + dz) % rows) * ROW + (x + dx) % ROW
                pairs.append((s * peers + z * ROW + x, (s + ds) * peers + there))
    return lax.ppermute(array, ("section", "peer"), pairs)


def along(axis, by):
    return (by, 0) if axis == "z" else (0, by)


def ring_gather(block, axis):
    half = block.shape[0] // 2
    ahead = move(block, *along(axis, 1))
    behind = move(block, *along(axis, -1))
    far_low = move(ahead[:half], *along(axis, 1))
    far_high = move(behind[half:], *along(axis, -1))
    return [(0, 0, block), (-1, 0, ahead), (1, 0, behind), (2, 0, far_low), (2, half, far_high)]


OFFSETS = (0, -1, 1, 2)


def near_gather(piece, axis):
    return jnp.concatenate([piece] + [move(piece, *along(axis, -offset)) for offset in OFFSETS[1:]], axis=0)


def far_gather(lead, axis, parts):
    rows = lead.shape[0] // ROW
    held = []
    for far, row, block in ring_gather(lead, axis):
        spans = []
        for i in range(block.shape[0] // rows):
            near = OFFSETS[row // rows + i]
            dz, dx = (near, far) if axis == "x" else (far, near)
            at = i * rows
            for layer, start, count in parts:
                spans.append((at, dz, dx, layer, start, count))
                at += count
        held.append((block, spans))
    return held


def put_together(full_refs, refs, spans, where_ref, share, sems):
    copies = [[] for _ in full_refs]
    count = 0
    for ref, held in zip(refs, spans, strict=True):
        for row, dz, dx, layer, start, rows in held:
            z = lax.rem(where_ref[0] + (dz + ROW), ROW)
            x = lax.rem(where_ref[1] + (dx + ROW), ROW)
            there = pl.multiple_of((z * ROW + x) * share + start, 16)
            copy = pltpu.make_async_copy(
                ref.at[pl.ds(row, rows), :], full_refs[layer].at[pl.ds(there, rows), :], sems.at[count]
            )
            copy.start()
            copies[layer].append(copy)
            count += 1
    return copies


def wait_all(copies):
    for copy in copies:
        copy.wait()


def loop(steps, body, carry):
    for step in range(steps):
        carry = body(step, carry)
    return carry


def columns(step):
    return slice(step * CHUNK, (step + 1) * CHUNK)


def dot(left, right):
    return jnp.dot(left, right, preferred_element_type=jnp.float32)


def dot_cols(left, right):
    return lax.dot_general(left, right, (((1,), (1,)), ((), ())), preferred_element_type=jnp.float32)


def dot_rows(left, right):
    return lax.dot_general(left, right, (((0,), (0,)), ((), ())), preferred_element_type=jnp.float32)


def inverse_norm(stream_ref):
    rows, width = stream_ref.shape

    def add(step, total):
        part = stream_ref[:, columns(step)].astype(jnp.float32)
        return total + jnp.sum(part * part, axis=-1, keepdims=True)

    total = loop(width // CHUNK, add, jnp.zeros((rows, 1), jnp.float32))
    return lax.rsqrt(total / width + EPS)


def project(stream_ref, inverse, gain_ref, layer, full_ref):
    rows, width = stream_ref.shape
    rank = full_ref.shape[1] // 3

    def add(step, total):
        cols = columns(step)
        normed = stream_ref[:, cols].astype(jnp.float32) * inverse
        scaled = (normed * gain_ref[layer : layer + 1, cols]).astype(jnp.bfloat16)
        return total + dot(scaled, full_ref[cols, : 2 * rank])

    return loop(width // CHUNK, add, jnp.zeros((rows, 2 * rank), jnp.float32))


def gate(projected):
    rank = projected.shape[1] // 2
    upward, gating = projected[:, :rank], projected[:, rank:]
    sigmoid = jax.nn.sigmoid(gating)
    hidden = (gating * sigmoid * upward).astype(jnp.bfloat16)
    return upward, gating, sigmoid, hidden


def step_back(d_hidden, projected):
    upward, gating, sigmoid, hidden = gate(projected)
    d_upward = d_hidden * (gating * sigmoid)
    d_gating = d_hidden * upward * sigmoid * (1.0 + gating * (1.0 - sigmoid))
    return jnp.concatenate([d_upward, d_gating], axis=-1).astype(jnp.bfloat16), hidden


def hand_out(index_ref, rows_ref, routed_ref, slots):
    for peer in range(routed_ref.shape[0]):
        index = index_ref[peer]

        @pl.when(index >= 0)
        def _(index=index, peer=peer):
            start = pl.multiple_of(jnp.maximum(index, 0) * slots, slots)
            routed_ref[peer] = rows_ref[pl.ds(start, slots), :]

        @pl.when(index < 0)
        def _(peer=peer):
            routed_ref[peer] = jnp.zeros((slots, rows_ref.shape[1]), rows_ref.dtype)


def forward_kernel(spans, share, where_ref, gain_ref, input_ref, *refs):
    blocks = refs[: len(spans)]
    rows_ref, low_full_ref, high_full_ref, stream_ref, sems = refs[len(spans) :]
    copies = put_together((low_full_ref, high_full_ref), blocks, spans, where_ref, share, sems)
    rank = low_full_ref.shape[1] // 3
    steps = input_ref.shape[1] // CHUNK
    inverse = inverse_norm(input_ref)
    wait_all(copies[0])
    hidden = gate(project(input_ref, inverse, gain_ref, 0, low_full_ref))[3]

    def lower(step, total):
        cols = columns(step)
        new = input_ref[:, cols].astype(jnp.float32) + dot_cols(hidden, low_full_ref[cols, 2 * rank :])
        stream_ref[:, cols] = new
        return total + jnp.sum(new * new, axis=-1, keepdims=True)

    total = loop(steps, lower, jnp.zeros((input_ref.shape[0], 1), jnp.float32))
    inverse = lax.rsqrt(total / input_ref.shape[1] + EPS)
    wait_all(copies[1])
    hidden_high = gate(project(stream_ref, inverse, gain_ref, 1, high_full_ref))[3]

    def upper(step, carry):
        cols = columns(step)
        new = stream_ref[:, cols] + dot_cols(hidden_high, high_full_ref[cols, 2 * rank :])
        rows_ref[:, cols] = new.astype(jnp.bfloat16)
        return carry

    loop(steps, upper, 0)


def spread_kernel(slots, index_ref, rows_ref, routed_ref):
    hand_out(index_ref, rows_ref, routed_ref, slots)


def back_kernel(spans, share, where_ref, gain_ref, saved_ref, cot_ref, *refs):
    blocks, refs = refs[: len(spans)], refs[len(spans) :]
    rows_ref, own_ref, up_ref, down_ref, next_ref, last_ref = refs[:6]
    low_full_ref, high_full_ref, stream_ref, scaled_ref, cot_low_ref, cot_high_ref, grad_ref, sems = refs[6:]
    copies = put_together((low_full_ref, high_full_ref), blocks, spans, where_ref, share, sems)
    count, width = saved_ref.shape
    rank = low_full_ref.shape[1] // 3
    steps = width // CHUNK
    f32, bf16 = jnp.float32, jnp.bfloat16
    nothing = jnp.zeros((count, rank), f32)

    inverse_low = inverse_norm(saved_ref)
    wait_all(copies[0])
    projected_low = project(saved_ref, inverse_low, gain_ref, 0, low_full_ref)
    hidden_low = gate(projected_low)[3]

    def first(step, total):
        cols = columns(step)
        new = saved_ref[:, cols].astype(f32) + dot_cols(hidden_low, low_full_ref[cols, 2 * rank :])
        stream_ref[:, cols] = new
        return total + jnp.sum(new * new, axis=-1, keepdims=True)

    total = loop(steps, first, jnp.zeros((count, 1), f32))
    inverse = lax.rsqrt(total / width + EPS)
    wait_all(copies[1])

    def forward(step, carry):
        projected, d_hidden = carry
        cols = columns(step)
        scaled = (stream_ref[:, cols] * inverse * gain_ref[1:2, cols]).astype(bf16)
        scaled_ref[:, cols] = scaled
        projected = projected + dot(scaled, high_full_ref[cols, : 2 * rank])
        d_hidden = d_hidden + dot(cot_ref[:, cols], high_full_ref[cols, 2 * rank :])
        return projected, d_hidden

    projected, d_hidden = loop(
        steps, forward, (jnp.zeros((count, 2 * rank), f32), nothing)
    )
    d_projected, hidden = step_back(d_hidden, projected)
    inner = jnp.sum(d_projected.astype(f32) * projected, axis=-1, keepdims=True) / width

    def store_grad(layer, step, scaled, cot_low, d_projected, hidden):
        peer = step * (CHUNK // share)
        wide = dot_rows(scaled, d_projected).astype(bf16)
        down = dot_rows(cot_low, hidden).astype(bf16)
        for i in range(CHUNK // share):
            grad_ref[layer, peer + i, :, : 2 * rank] = wide[i * share : (i + 1) * share]
            grad_ref[layer, peer + i, :, 2 * rank :] = down[i * share : (i + 1) * share]

    def upper(step, d_hidden_low):
        cols = columns(step)
        d_normed = dot_cols(d_projected, high_full_ref[cols, : 2 * rank]) * gain_ref[1:2, cols]
        normed = stream_ref[:, cols] * inverse
        cot_low = cot_ref[:, cols]
        new = cot_low.astype(f32) + inverse * (d_normed - normed * inner)
        cot_high_ref[:, cols] = new
        low = new.astype(bf16)
        cot_low_ref[:, cols] = low
        store_grad(1, step, scaled_ref[:, cols], cot_low, d_projected, hidden)
        return d_hidden_low + dot(low, low_full_ref[cols, 2 * rank :])

    d_hidden_low = loop(steps, upper, nothing)
    d_projected_low, _ = step_back(d_hidden_low, projected_low)
    inner_low = jnp.sum(d_projected_low.astype(f32) * projected_low, axis=-1, keepdims=True) / width

    def lower(step, carry):
        cols = columns(step)
        gain = gain_ref[0:1, cols]
        d_normed = dot_cols(d_projected_low, low_full_ref[cols, : 2 * rank]) * gain
        normed = saved_ref[:, cols].astype(f32) * inverse_low
        new = cot_high_ref[:, cols] + inverse_low * (d_normed - normed * inner_low)
        rows_ref[:, cols] = new.astype(bf16)
        scaled = (normed * gain).astype(bf16)
        store_grad(0, step, scaled, cot_low_ref[:, cols], d_projected_low, hidden_low)
        return carry

    loop(steps, lower, 0)

    half = share // 2
    for layer in range(2):
        for dz in range(ROW):
            z = lax.rem(where_ref[0] + dz, ROW) * ROW
            own, ahead, far, behind = (z + lax.rem(where_ref[1] + dx, ROW) for dx in range(ROW))
            own_ref[dz, layer] = grad_ref[layer, own]
            up_ref[0, dz, layer] = grad_ref[layer, far, :half]
            up_ref[1, dz, layer] = grad_ref[layer, ahead, half:]
            down_ref[0, dz, layer] = grad_ref[layer, far, half:]
            down_ref[1, dz, layer] = grad_ref[layer, behind, :half]
            next_ref[dz, layer] = grad_ref[layer, ahead, :half]
            last_ref[dz, layer] = grad_ref[layer, behind, half:]


def vmem(count):
    return [pl.BlockSpec(memory_space=pltpu.VMEM)] * count


def smem(count):
    return [pl.BlockSpec(memory_space=pltpu.SMEM)] * count


def shaped(*shape, dtype=jnp.bfloat16):
    return jax.ShapeDtypeStruct(shape, dtype)


def exchange(routed):
    return lax.all_to_all(routed, "peer", split_axis=0, concat_axis=0, tiled=True)


def settle_kernel(from_ref, to_ref):
    to_ref[...] = from_ref[...]


def settle(array):
    step = pl.BlockSpec((2,) + array.shape[1:], lambda i: (i, 0, 0))
    return pl.pallas_call(
        settle_kernel,
        out_shape=jax.ShapeDtypeStruct(array.shape, array.dtype),
        grid=(array.shape[0] // 2,),
        in_specs=[step],
        out_specs=step,
        cost_estimate=cost(3),
    )(array)


def slots_of(targets, active):
    names = jnp.arange(lax.axis_size("peer"), dtype=jnp.int32)
    table = (targets[:, None] == names[None, :]) & active
    micro = jnp.arange(targets.shape[0], dtype=jnp.int32)
    return jnp.max(jnp.where(table, micro[:, None], -1), axis=0)


def add_up(*terms):
    total = terms[0].astype(jnp.float32)
    for term in terms[1:]:
        total = total + term.astype(jnp.float32)
    return total


def scatter_first(up, down, axis):
    return move(up, *along(axis, 1)), move(down, *along(axis, -1))


def scatter_rest(own, ahead, behind, got_up, got_down, axis):
    half = ahead.shape[-2]
    ahead = add_up(ahead, got_up[0]).astype(own.dtype)
    behind = add_up(behind, got_down[0]).astype(own.dtype)
    ahead, behind = lax.optimization_barrier((ahead, behind))
    got_ahead, got_behind = move(ahead, *along(axis, 1)), move(behind, *along(axis, -1))
    low = add_up(own[..., :half, :], got_ahead, got_down[1])
    high = add_up(own[..., half:, :], got_behind, got_up[1])
    return low, high


def reduce_scatter(own, ahead, behind, got_up, got_down, after):
    dtype = own.dtype
    low, high = scatter_rest(own, ahead, behind, got_up, got_down, "x")
    low, high = low.astype(dtype), high.astype(dtype)
    up, down = scatter_first(jnp.stack([low[2], high[1]]), jnp.stack([high[2], low[3]]), "z")
    up, down, after = lax.optimization_barrier((up, down, after))
    mine = jnp.concatenate([low[0], high[0]], axis=1)
    return jnp.concatenate(scatter_rest(mine, low[1], high[3], up, down, "z"), axis=1), after


def cost(micros):
    return pl.CostEstimate(flops=micros * 10**9, bytes_accessed=micros * 3 * 10**6, transcendentals=0)


def per_device(
    forward_inputs,
    saved_inputs,
    cotangents,
    lengths,
    peer_counts,
    wiring,
    back_wiring,
    norm_gains,
    in_weights,
    down_weights,
):
    section_id = lax.axis_index("section")
    peer_id = lax.axis_index("peer")
    where = jnp.stack([peer_id // ROW, peer_id % ROW]).astype(jnp.int32)
    active = peer_id < peer_counts[section_id]
    micro, slots, width = forward_inputs.shape[2:]
    count = micro * slots
    rank = down_weights.shape[2]
    share = in_weights.shape[2]
    gains = norm_gains[0]
    f32 = jnp.float32

    both = jnp.concatenate([in_weights[0], jnp.swapaxes(down_weights[0], 1, 2)], axis=-1)
    cut = share * 45 // 100 // 16 * 16
    by_z = near_gather(jnp.concatenate([both[0], both[1, :cut]], axis=0), "z")
    by_x = near_gather(both[1, cut:], "x")
    forward_slots = move(slots_of(wiring[0, 0], active), 0, 0, 1)
    back_slots = move(slots_of(back_wiring[0, 0], active), 0, 0, -1)
    by_z, by_x, forward_slots, back_slots = lax.optimization_barrier((by_z, by_x, forward_slots, back_slots))
    blocks = far_gather(by_z, "x", [(0, 0, share), (1, 0, cut)])
    blocks += far_gather(by_x, "z", [(1, cut, share - cut)])

    positions = jnp.arange(slots, dtype=jnp.int32)
    live = (positions[None, :] < lengths[0, 0][:, None]) & active
    cot = jnp.where(live[:, :, None], cotangents[0, 0], jnp.zeros((), cotangents.dtype))
    cot = cot.reshape(count, width)
    saved = saved_inputs.reshape(count, width)

    peers = ROW * ROW
    routed = shaped(peers, slots, width)
    flat = shaped(count, width)
    bf16 = jnp.bfloat16

    spans = [held for _, held in blocks]
    arrays = [array for array, _ in blocks]
    anywhere = [pl.BlockSpec(memory_space=pl.ANY)] * len(spans)
    wide = [pltpu.VMEM((width, 3 * rank), bf16)] * 2
    sems = pltpu.SemaphoreType.DMA((sum(len(held) for held in spans),))
    rows = pl.pallas_call(
        functools.partial(forward_kernel, spans, share),
        out_shape=flat,
        in_specs=smem(1) + vmem(2) + anywhere,
        out_specs=vmem(1)[0],
        scratch_shapes=wide + [pltpu.VMEM((count, width), f32), sems],
        compiler_params=pltpu.CompilerParams(vmem_limit_bytes=40 << 20),
        cost_estimate=cost(12),
    )(where, gains, forward_inputs.reshape(count, width), *arrays)

    rows, saved = lax.optimization_barrier((rows, saved))

    def spread(index, rows):
        return pl.pallas_call(
            functools.partial(spread_kernel, slots),
            out_shape=routed,
            in_specs=smem(1) + vmem(1),
            out_specs=vmem(1)[0],
            compiler_params=pltpu.CompilerParams(vmem_limit_bytes=16 << 20),
            cost_estimate=cost(2),
        )(index, rows)

    shifted = move(rows, 0, 0, 1)

    part = shaped(ROW, 2, share // 2, 3 * rank)
    pair = shaped(2, ROW, 2, share // 2, 3 * rank)
    d_rows, own, up, down, ahead, behind = pl.pallas_call(
        functools.partial(back_kernel, spans, share),
        out_shape=[flat, shaped(ROW, 2, share, 3 * rank), pair, pair, part, part],
        in_specs=smem(1) + vmem(3) + anywhere,
        out_specs=vmem(6),
        scratch_shapes=wide
        + [
            pltpu.VMEM((count, width), f32),
            pltpu.VMEM((count, width), bf16),
            pltpu.VMEM((count, width), bf16),
            pltpu.VMEM((count, width), f32),
            pltpu.VMEM((2, peers, share, 3 * rank), bf16),
            sems,
        ],
        compiler_params=pltpu.CompilerParams(vmem_limit_bytes=52 << 20),
        cost_estimate=cost(25),
    )(where, gains, saved, cot, *arrays)
    shifted, d_rows, up, down = lax.optimization_barrier((shifted, d_rows, up, down))
    got_up, got_down = scatter_first(up, down, "x")
    forward_arrived = settle(exchange(spread(forward_slots, shifted)))
    returned = spread(back_slots, move(d_rows, 0, 0, -1))
    returned, got_up, got_down = lax.optimization_barrier((returned, got_up, got_down))
    backward_arrived = exchange(returned)
    total, forward_arrived = reduce_scatter(own, ahead, behind, got_up, got_down, forward_arrived)

    grad_in = total[:, :, : 2 * rank]
    grad_down = jnp.swapaxes(total[:, :, 2 * rank :], 1, 2)
    return (
        forward_arrived.reshape(1, 1, peers, slots, width),
        backward_arrived.reshape(1, 1, peers, slots, width),
        grad_in[None],
        grad_down[None],
    )


def solution(mesh):
    return jax.shard_map(
        per_device,
        mesh=mesh,
        in_specs=(
            P("section", "peer", None, None, None),
            P("section", "peer", None, None, None),
            P("section", "peer", None, None, None),
            P("section", "peer", None),
            P(),
            P("section", "peer", None),
            P("section", "peer", None),
            P("section", None, None),
            P("section", None, "peer", None),
            P("section", None, None, "peer"),
        ),
        out_specs=(
            P("section", "peer", None, None, None),
            P("section", "peer", None, None, None),
            P("section", None, "peer", None),
            P("section", None, None, "peer"),
        ),
        check_vma=False,
    )
```
